32 devices in a mesh: sx: 4 (over y, x), sy: 4 (over z), freq: 2 (over core).
Axes of the slice: x: 2, y: 2, z: 4, core: 2. Of those that a mesh axis runs over, the one named last changes fastest.
Arguments:
- update_basis: bfloat16 [4, 512, 32, 1024], P('freq', ('sx', 'sy')), may hold values from -0.1875 to 0.1875
- update_coeff: bfloat16 [4, 512, 32, 128], P('freq', ('sx', 'sy')), may hold values from -6 to 6
- owner: int32 [512, 1], P(('sx', 'sy')), may hold values from 0 to 3; in each aligned block of 32 rows (0 to 31, 32 to 63, ...) at most 16 rows name the same one
- sep_rhs: bfloat16 [4, 4, 4, 1024, 128], P('freq', 'sx', 'sy'), may hold values from -6 to 6
- coupling: float32 [4, 4, 4, 4, 1024], P('freq', 'sx', 'sy'), may hold values from 0.1 to 0.25
- frontal_inverse: bfloat16 [4, 4, 4, 1024, 1024], P('freq', 'sx', 'sy'), may hold values from -0.2 to 1.2
Outputs:
- solution: float32 [4, 4, 4, 1024, 128], P('freq', 'sx', 'sy')
- residual_total: float32 [], replicated
The draws below stay inside these ranges and needn't reach their ends.
Inputs may be any that keep to these rules, and one draw needn't show every extreme that they name: In the 32 children of one grid position no owner appears more than 16 times; in every draw some owner appears exactly 16 times at some position.
All inputs are finite; a program needn't handle non-finite values.
Results may differ from the reference program's by a relative error of at most 0.0019.
Values may be sent and summed in bfloat16 or wider, within the bound.
A program may use at most 128 MiB of HBM per device.

```python
import math
import jax
import jax.numpy as jnp
import numpy as np
from jax import lax

SEP = 1024
RANK = 32
NRHS = 128
C_DEV = 32
SWEEPS = 2
GRID_X = 4
GRID_Y = 4
CHILDREN = 512
FREQS = 4
CAP = 16
N_SX = 4


def draw_frontal_inverse(key, part):
    first_key, second_key = jax.random.split(jax.random.fold_in(key, 7))
    spread = 0.35 * math.sqrt(3.0) / math.sqrt(SEP)
    matrix = jax.random.uniform(first_key, (FREQS, GRID_X, GRID_Y, SEP, SEP), jnp.float32, -spread, spread)
    diagonal = jax.random.uniform(second_key, (FREQS, GRID_X, GRID_Y, SEP), jnp.float32, 0.7, 0.9)
    positions = jnp.arange(SEP, dtype=jnp.int32)
    matrix = matrix.at[:, :, :, positions, positions].add(diagonal)
    return matrix.astype(jnp.bfloat16)


def block_scale(own_key, dims, pieces, low, top_value):
    factor_of = 1.0
    for dim, blocks in pieces:
        heights = jax.random.uniform(jax.random.fold_in(jax.random.fold_in(own_key, 6), dim), (blocks,), jnp.float32, low / len(pieces), top_value / len(pieces))
        factor_of = factor_of * jnp.repeat(jnp.exp(heights), dims[dim] // blocks).reshape((-1,) + (1,) * (len(dims) - 1 - dim))
    return factor_of


def shared_out(own_key, own, number, rows, amount, top, reach, lean):
    sequence = jax.random.permutation(own_key, amount)
    heavy_load, ordinary = load_shares(amount, rows * top, reach, lean, True), load_shares(amount, rows * top, reach, lean, False)
    places = jnp.arange(amount)

    def named(lengths, offset_by):
        used = int((lengths > 0).sum())
        fixed = max(1, used // 4)
        passed = fixed + (places - fixed + offset_by * (used - fixed)) % max(1, amount - fixed)
        return jnp.zeros((amount,), jnp.int32).at[sequence[jnp.where(places < fixed, places, passed)]].set(jnp.asarray(lengths, jnp.int32))

    lengths = jnp.where(number % 4 == 0, named(heavy_load, number // 4), named(ordinary, number - number // 4 - 1))
    mixed = jax.random.permutation(jax.random.fold_in(own, 3), amount)
    donor, receiver = mixed[0:amount // 2 * 2:2], mixed[1:amount // 2 * 2:2]
    margin = jnp.minimum(lengths[donor] - 1, reach - lengths[receiver]) // 2
    margin = jnp.where((donor == sequence[0]) | (receiver == sequence[0]) | (lengths[receiver] == 0), 0, jnp.maximum(margin, 0))
    passed = jax.random.randint(jax.random.fold_in(own, 4), (amount // 2,), 0, 1 << 20) % (margin + 1)
    lengths = lengths.at[donor].add(-passed).at[receiver].add(passed)
    members = jnp.searchsorted(jnp.cumsum(lengths), jnp.arange(rows * top), side="right").astype(jnp.int32)
    listing = members.reshape(top, rows).T
    listing = listing[jax.random.permutation(jax.random.fold_in(own, 1), rows)]
    offset_by = jax.random.randint(jax.random.fold_in(own, 2), (rows, 1), 0, top)
    return jnp.take_along_axis(listing, (jnp.arange(top)[None, :] + offset_by) % top, axis=1)


def load_shares(number_of, total, most, slope, full):
    weights = [(1 << 20) // math.isqrt(standing ** slope) + 1 for standing in range(1, number_of + 1)]
    largest = most if full else min(most, max(-(-total // number_of), total * weights[0] // sum(weights)))
    least = 1 if total - largest >= number_of - 1 else 0
    holding, rest = [largest] + [least] * (number_of - 1), total - largest - least * (number_of - 1)
    while rest > 0:
        free = [i for i in range(1, number_of) if holding[i] < largest] or [i for i in range(1, number_of) if holding[i] < most]
        pool, remaining = sum([weights[i] for i in free]), rest
        for i in free:
            more = min(most - holding[i], max(1, remaining * weights[i] // pool), rest)
            holding[i] = holding[i] + more
            rest = rest - more
    return np.array(holding)


def bell_draw(rng, dims, scale, bound, pieces=(), held_as=jnp.bfloat16):
    drawn = scale * jax.random.normal(rng, dims, jnp.float32)
    if pieces:
        drawn = drawn * block_scale(rng, dims, pieces, -0.22, 0.18)
    return jnp.clip(drawn, -bound, bound).astype(held_as)


def setup_inputs(seed: int = 0) -> dict:
    streams_of = jax.random.split(jax.random.key(seed), 7)
    update_basis = bell_draw(streams_of[0], (FREQS, CHILDREN, RANK, SEP), (RANK * C_DEV) ** -0.5, 0.1875, ((0, 2), (1, 16)))
    update_coeff = bell_draw(streams_of[1], (FREQS, CHILDREN, RANK, NRHS), 1.0, 6.0, ((0, 2), (1, 16)))
    owner_keys = jax.random.split(jax.random.fold_in(streams_of[2], 1), CHILDREN // C_DEV)
    owner_turns = jax.random.permutation(jax.random.fold_in(streams_of[2], 3), CHILDREN // C_DEV)
    owner = jax.vmap(lambda own, number: shared_out(jax.random.fold_in(streams_of[2], 2), own, number, C_DEV, N_SX, 1, CAP, 2))(owner_keys, owner_turns).reshape((CHILDREN, 1))
    sep_rhs = bell_draw(streams_of[3], (FREQS, GRID_X, GRID_Y, SEP, NRHS), 1.0, 6.0, ((0, 2), (1, 4), (2, 4)))
    coupling = jnp.clip(0.1 + 0.15 * jax.random.uniform(streams_of[4], (FREQS, GRID_X, GRID_Y, 4, SEP), jnp.float32) ** block_scale(streams_of[4], (FREQS, GRID_X, GRID_Y, 4, SEP), ((0, 2), (1, 4), (2, 4)), -0.2, 0.2), 0.1, 0.25)
    frontal_inverse = draw_frontal_inverse(jax.random.fold_in(streams_of[6], 71), 0)
    return dict(update_basis=update_basis, update_coeff=update_coeff, owner=owner, sep_rhs=sep_rhs, coupling=coupling, frontal_inverse=frontal_inverse)


def apply_inverse(frontal_inverse, field):
    rounded = lax.optimization_barrier(field.astype(jnp.bfloat16))

    def one_frequency(pair):
        matrix, vectors = pair
        return jnp.einsum('xyst,xytn->xysn', matrix.astype(jnp.float32), vectors.astype(jnp.float32))
    return lax.map(one_frequency, (frontal_inverse, rounded))

def neighbour_sum(field, coupling):
    padded = jnp.pad(field, ((0, 0), (1, 1), (1, 1), (0, 0), (0, 0)))
    result = coupling[:, :, :, 0, :, None] * padded[:, :-2, 1:-1]
    result = result + coupling[:, :, :, 1, :, None] * padded[:, 2:, 1:-1]
    result = result + coupling[:, :, :, 2, :, None] * padded[:, 1:-1, :-2]
    result = result + coupling[:, :, :, 3, :, None] * padded[:, 1:-1, 2:]
    return result

def reference(update_basis, update_coeff, owner, sep_rhs, coupling, frontal_inverse):
    blocks = CHILDREN // C_DEV
    owners = owner[:, 0].reshape(blocks, C_DEV)
    accumulated = jnp.zeros((FREQS, GRID_X, GRID_Y, SEP, NRHS), jnp.float32)

    def add_block(total, block_index):
        start = block_index * C_DEV
        basis_block = lax.dynamic_slice_in_dim(update_basis, start, C_DEV, 1).astype(jnp.float32)
        coeff_block = lax.dynamic_slice_in_dim(update_coeff, start, C_DEV, 1).astype(jnp.float32)
        products = jnp.einsum('fcrs,fcrn->fcsn', basis_block, coeff_block)
        targets = lax.dynamic_index_in_dim(owners, block_index, 0, keepdims=False)
        column = block_index % GRID_Y
        total = total.at[:, targets, column].add(products)
        return (total, None)
    accumulated, unused = lax.scan(add_block, accumulated, jnp.arange(blocks, dtype=jnp.int32))
    right_side = sep_rhs.astype(jnp.float32) - accumulated
    solution = apply_inverse(frontal_inverse, right_side)
    residual = right_side
    for sweep_index in range(SWEEPS):
        residual = right_side - solution + neighbour_sum(solution, coupling)
        solution = solution + apply_inverse(frontal_inverse, residual)
    weights = (jnp.arange(FREQS, dtype=jnp.float32) + 1.0) ** 2
    weighted_sum = jnp.sum(weights * lax.optimization_barrier(jnp.sum(residual * residual, axis=(1, 2, 3, 4))))
    residual_total = jnp.sqrt(weighted_sum / (FREQS * GRID_X * GRID_Y * SEP * NRHS) + 1e-06)
    return (solution, residual_total)
```

```python
import functools
import jax
import jax.numpy as jnp
from jax import lax
from jax.experimental import pallas as pl
from jax.experimental.pallas import tpu as pltpu
from jax.sharding import PartitionSpec as P

SWEEPS = 2
BLOCK = 256
GROUP = 512
MESH = pl.DeviceIdType.MESH
F32 = jnp.float32
BF16 = jnp.bfloat16


def kernel(
    sizes,
    basis_hbm, coeff_ref, owner_ref, rhs_ref, coupling_ref, inverse_hbm,
    out_ref, total_ref,
    basis_ref, inverse_ref, masked_ref, sent_ref, got_ref, own_ref, right_ref, field_ref,
    halo_out_ref, halo_in_ref, coupling_t_ref, sums_a_ref, sums_b_ref,
    basis_sem, inverse_sem, sent_sem, got_sem, halo_out_sem, halo_in_sem,
    a_send_sem, a_recv_sem, b_send_sem, b_recv_sem,
):
    n_x, n_y, n_f, entries = sizes
    f_local, depth, sep = basis_ref.shape
    rhs_count = rhs_ref.shape[2]
    children = owner_ref.shape[0]
    rank = depth // children
    blocks = sep // BLOCK
    paired = n_x == 4
    x = lax.axis_index("sx")
    y = lax.axis_index("sy")
    z = lax.axis_index("freq")

    loads = []
    for f in range(f_local):
        loads.append(pltpu.make_async_copy(basis_hbm.at[f], basis_ref.at[f], basis_sem.at[f]))
    inverse_loads = []
    for f in range(f_local):
        inverse_loads.append(
            pltpu.make_async_copy(inverse_hbm.at[f], inverse_ref.at[f], inverse_sem.at[f])
        )
    for copy in loads + inverse_loads:
        copy.start()

    barrier = pltpu.get_barrier_semaphore()
    count = 0
    for dx in range(n_x):
        for dz in range(n_f):
            if dx or dz:
                pl.semaphore_signal(
                    barrier, inc=1, device_id=(lax.rem(x + dx, n_x), y, lax.rem(z + dz, n_f)),
                    device_id_type=MESH,
                )
                count += 1
    for dy in range(1, n_y):
        pl.semaphore_signal(
            barrier, inc=1, device_id=(x, lax.rem(y + dy, n_y), z), device_id_type=MESH
        )
        count += 1

    if paired:
        px, py = lax.rem(x, 2), x // 2
        owners = [(1 - py) * 2 + 1 - px, py * 2 + 1 - px, (1 - py) * 2 + px, x]
    else:
        owners = [lax.rem(x + k, n_x) for k in range(1, n_x)] + [x]

    def mask(f):
        def one_child(c, carry):
            mine = owner_ref[pl.ds(c, 1), :]
            rows = pl.ds(pl.multiple_of(c * rank, rank), rank)
            values = coeff_ref[f, rows, :]
            for k, who in enumerate(owners):
                keep = jnp.where(mine == who, 1.0, 0.0).astype(F32)
                keep = jnp.broadcast_to(keep, (rank, rhs_count)).astype(BF16)
                masked_ref[f, rows, k * rhs_count:(k + 1) * rhs_count] = values * keep
            return carry

        lax.fori_loop(0, children, one_child, 0, unroll=4)

    pending = []

    def remote(src, dst, send, recv, device):
        return pltpu.make_async_remote_copy(
            src_ref=src, dst_ref=dst, send_sem=send, recv_sem=recv,
            device_id=device, device_id_type=MESH,
        )

    def sum_copy(f, k, b):
        rows = pl.ds(b * BLOCK, BLOCK)
        return remote(
            sent_ref.at[k, f, rows], got_ref.at[k, f, rows],
            sent_sem.at[k, f, b], got_sem.at[k, f, b], (owners[k], y, z),
        )

    for f in range(f_local):
        mask(f)
        loads[f].wait()
        if f == 0:
            pl.semaphore_wait(barrier, count)
        for b in range(blocks):
            rows = pl.ds(b * BLOCK, BLOCK)
            part = basis_ref[f, :, b * BLOCK:(b + 1) * BLOCK]
            for low in range(0, n_x * rhs_count, GROUP):
                high = min(low + GROUP, n_x * rhs_count)
                sums = lax.dot_general(
                    part, masked_ref[f, :, low:high], (((0,), (0,)), ((), ())),
                    preferred_element_type=F32,
                )
                for k in range(low // rhs_count, high // rhs_count):
                    at = k * rhs_count - low
                    piece = sums[:, at:at + rhs_count]
                    if k == n_x - 1:
                        own_ref[f, rows, :] = rhs_ref[f, rows, :].astype(F32) - piece
                    else:
                        sent_ref[k, f, rows, :] = piece.astype(BF16)
                        copy = sum_copy(f, k, b)
                        copy.start()
                        pending.append((None, copy))

    both = jnp.concatenate([coupling_ref[f] for f in range(f_local)], axis=0)
    coupling_t_ref[...] = both.T

    edges = ((x == 0, 0), (x == n_x - 1, 1), (y == 0, 2), (y == n_y - 1, 3))
    for missing, side in edges:
        @pl.when(missing)
        def _():
            for sweep in range(SWEEPS):
                for f in range(f_local):
                    halo_in_ref[sweep, f, side] = jnp.zeros((sep, rhs_count), BF16)

    def halo_copy(sweep, f, b, way, source, device):
        rows = pl.ds(b * BLOCK, BLOCK)
        return remote(
            source, halo_in_ref.at[sweep, f, way, rows],
            halo_out_sem.at[sweep, f, way, b], halo_in_sem.at[sweep, f, way, b], device,
        )

    up, down = x < n_x - 1, x > 0
    if paired:
        up = jnp.logical_and(up, x != 1)
        down = jnp.logical_and(down, x != 2)

    def send_halo(sweep, f, b):
        source = halo_out_ref.at[sweep, f, pl.ds(b * BLOCK, BLOCK)]
        for way, test, device in (
            (0, up, (x + 1, y, z)), (1, down, (x - 1, y, z)),
            (2, y < n_y - 1, (x, y + 1, z)), (3, y > 0, (x, y - 1, z)),
        ):
            copy = halo_copy(sweep, f, b, way, source, device)
            pl.when(test)(copy.start)
            pending.append((test, copy))

    def wait_halo(sweep, f, b, way):
        source = halo_out_ref.at[sweep, f, pl.ds(b * BLOCK, BLOCK)]
        test = (x > 0, x < n_x - 1, y > 0, y < n_y - 1)[way]
        copy = halo_copy(sweep, f, b, way, source, (x, y, z))
        pl.when(test)(copy.wait_recv)

    def pass_on(sweep, f, b):
        rows = pl.ds(b * BLOCK, BLOCK)
        for test, held, way, target in ((x == 0, 1, 0, 2), (x == 3, 0, 1, 1)):
            source = halo_in_ref.at[sweep, f, held, rows]
            copy = remote(
                source, halo_in_ref.at[sweep, f, way, rows],
                halo_out_sem.at[sweep, f, held, b], halo_in_sem.at[sweep, f, way, b],
                (target, y, z),
            )
            pl.when(test)(copy.start)
            pending.append((test, copy))

    def apply_inverse(f, sweep, first):
        for b in range(blocks):
            rows = pl.ds(b * BLOCK, BLOCK)
            value = jnp.dot(inverse_ref[f, rows, :], field_ref[f], preferred_element_type=F32)
            if not first:
                value = out_ref[f, rows, :] + value
            out_ref[f, rows, :] = value
            if sweep < SWEEPS:
                halo_out_ref[sweep, f, rows, :] = value.astype(BF16)
                send_halo(sweep, f, b)

    for f in range(f_local):
        for b in range(blocks):
            rows = pl.ds(b * BLOCK, BLOCK)
            value = own_ref[f, rows, :]
            for k in range(n_x - 1):
                sum_copy(f, k, b).wait_recv()
                value = value - got_ref[k, f, rows, :].astype(F32)
            right_ref[f, rows, :] = value
            field_ref[f, rows, :] = value.astype(BF16)
        inverse_loads[f].wait()
        apply_inverse(f, 0, True)

    weighted = jnp.zeros((8, rhs_count), F32)
    for sweep in range(SWEEPS):
        for f in range(f_local):
            for b in range(blocks):
                wait_halo(sweep, f, b, 0)
                wait_halo(sweep, f, b, 1)
                if paired:
                    pass_on(sweep, f, b)
            squares = jnp.zeros((8, rhs_count), F32)
            for b in range(blocks):
                wait_halo(sweep, f, b, 2)
                wait_halo(sweep, f, b, 3)
                rows = pl.ds(b * BLOCK, BLOCK)
                beside = jnp.zeros((BLOCK, rhs_count), F32)
                for side in range(4):
                    column = 4 * f + side
                    beside = beside + (
                        coupling_t_ref[rows, column:column + 1]
                        * halo_in_ref[sweep, f, side, rows, :].astype(F32)
                    )
                residual = right_ref[f, rows, :] - out_ref[f, rows, :] + beside
                field_ref[f, rows, :] = residual.astype(BF16)
                if sweep == SWEEPS - 1:
                    squares = squares + jnp.sum(
                        (residual * residual).reshape(BLOCK // 8, 8, rhs_count), axis=0
                    )
            if sweep == SWEEPS - 1:
                weight = (z * f_local + f + 1).astype(F32)
                weighted = weighted + (weight * weight) * squares
                if f == f_local - 1:
                    mine = x * n_f + z
                    sums_a_ref[mine] = weighted
                    for dx in range(n_x):
                        for dz in range(n_f):
                            if dx or dz:
                                k = dx * n_f + dz
                                copy = remote(
                                    sums_a_ref.at[mine], sums_a_ref.at[mine],
                                    a_send_sem.at[k], a_recv_sem.at[k],
                                    (lax.rem(x + dx, n_x), y, lax.rem(z + dz, n_f)),
                                )
                                copy.start()
                                pending.append((None, copy))
            apply_inverse(f, sweep + 1, False)

    for k in range(1, n_x * n_f):
        dx, dz = k // n_f, k % n_f
        source = lax.rem(x + n_x - dx, n_x) * n_f + lax.rem(z + n_f - dz, n_f)
        remote(
            sums_a_ref.at[source], sums_a_ref.at[source], a_send_sem.at[k], a_recv_sem.at[k],
            (x, y, z),
        ).wait_recv()
    part = sums_a_ref[0]
    for k in range(1, n_x * n_f):
        part = part + sums_a_ref[k]
    sums_b_ref[y] = part
    for dy in range(1, n_y):
        copy = remote(
            sums_b_ref.at[y], sums_b_ref.at[y], b_send_sem.at[dy], b_recv_sem.at[dy],
            (x, lax.rem(y + dy, n_y), z),
        )
        copy.start()
        pending.append((None, copy))
    for dy in range(1, n_y):
        source = lax.rem(y + n_y - dy, n_y)
        remote(
            sums_b_ref.at[source], sums_b_ref.at[source], b_send_sem.at[dy], b_recv_sem.at[dy],
            (x, y, z),
        ).wait_recv()
    part = sums_b_ref[0]
    for k in range(1, n_y):
        part = part + sums_b_ref[k]
    whole = jnp.sum(jnp.sum(part, axis=1, keepdims=True), axis=0, keepdims=True)
    total_ref[...] = jnp.sqrt(whole / entries + 1e-06)

    for test, copy in pending:
        if test is None:
            copy.wait_send()
        else:
            pl.when(test)(copy.wait_send)


def on_device(sizes, update_basis, update_coeff, owner, sep_rhs, coupling, frontal_inverse):
    f_local, children, rank, sep = update_basis.shape
    rhs_count = update_coeff.shape[3]
    depth = children * rank
    n_x, n_y, n_f = sizes
    blocks = sep // BLOCK
    entries = float(f_local * n_f * n_x * n_y * sep * rhs_count)
    vmem = pl.BlockSpec(memory_space=pltpu.VMEM)
    anywhere = pl.BlockSpec(memory_space=pl.ANY)
    solved, total = pl.pallas_call(
        functools.partial(kernel, (n_x, n_y, n_f, entries)),
        out_shape=(
            jax.ShapeDtypeStruct((f_local, sep, rhs_count), F32),
            jax.ShapeDtypeStruct((1, 1), F32),
        ),
        in_specs=[anywhere, vmem, vmem, vmem, vmem, anywhere],
        out_specs=(vmem, vmem),
        scratch_shapes=[
            pltpu.VMEM((f_local, depth, sep), BF16),
            pltpu.VMEM((f_local, sep, sep), BF16),
            pltpu.VMEM((f_local, depth, n_x * rhs_count), BF16),
            pltpu.VMEM((n_x - 1, f_local, sep, rhs_count), BF16),
            pltpu.VMEM((n_x - 1, f_local, sep, rhs_count), BF16),
            pltpu.VMEM((f_local, sep, rhs_count), F32),
            pltpu.VMEM((f_local, sep, rhs_count), F32),
            pltpu.VMEM((f_local, sep, rhs_count), BF16),
            pltpu.VMEM((SWEEPS, f_local, sep, rhs_count), BF16),
            pltpu.VMEM((SWEEPS, f_local, 4, sep, rhs_count), BF16),
            pltpu.VMEM((sep, 4 * f_local), F32),
            pltpu.VMEM((n_x * n_f, 8, rhs_count), F32),
            pltpu.VMEM((n_y, 8, rhs_count), F32),
            pltpu.SemaphoreType.DMA((f_local,)),
            pltpu.SemaphoreType.DMA((f_local,)),
            pltpu.SemaphoreType.DMA((n_x - 1, f_local, blocks)),
            pltpu.SemaphoreType.DMA((n_x - 1, f_local, blocks)),
            pltpu.SemaphoreType.DMA((SWEEPS, f_local, 4, blocks)),
            pltpu.SemaphoreType.DMA((SWEEPS, f_local, 4, blocks)),
            pltpu.SemaphoreType.DMA((n_x * n_f,)),
            pltpu.SemaphoreType.DMA((n_x * n_f,)),
            pltpu.SemaphoreType.DMA((n_y,)),
            pltpu.SemaphoreType.DMA((n_y,)),
        ],
        compiler_params=pltpu.CompilerParams(
            collective_id=0, has_side_effects=True, vmem_limit_bytes=56 * 2**20
        ),
    )(
        update_basis.reshape(f_local, depth, sep),
        update_coeff.reshape(f_local, depth, rhs_count),
        owner,
        sep_rhs[:, 0, 0],
        coupling[:, 0, 0],
        frontal_inverse[:, 0, 0],
    )
    return (solved[:, None, None], total.reshape(()))


def solution(mesh):
    sizes = (mesh.shape["sx"], mesh.shape["sy"], mesh.shape["freq"])
    return jax.shard_map(
        functools.partial(on_device, sizes),
        mesh=mesh,
        in_specs=(
            P("freq", ("sx", "sy"), None, None),
            P("freq", ("sx", "sy"), None, None),
            P(("sx", "sy"), None),
            P("freq", "sx", "sy", None, None),
            P("freq", "sx", "sy", None, None),
            P("freq", "sx", "sy", None, None),
        ),
        out_specs=(P("freq", "sx", "sy", None, None), P()),
        check_vma=False,
    )
```

```python
import functools
import jax
import jax.numpy as jnp
from jax import lax
from jax.experimental import pallas as pl
from jax.experimental.pallas import tpu as pltpu
from jax.sharding import PartitionSpec as P

SWEEPS = 2
BLOCK = 256
GROUP = 512
MESH = pl.DeviceIdType.MESH
F32 = jnp.float32
BF16 = jnp.bfloat16


def kernel(
    sizes,
    basis_hbm, coeff_ref, owner_ref, rhs_ref, coupling_ref, inverse_hbm,
    out_ref, total_ref,
    basis_ref, inverse_ref, masked_ref, sent_ref, got_ref, own_ref, right_ref, field_ref,
    halo_out_ref, halo_in_ref, coupling_t_ref, sums_a_ref, sums_b_ref,
    basis_sem, inverse_sem, sent_sem, got_sem, halo_out_sem, halo_in_sem,
    a_send_sem, a_recv_sem, b_send_sem, b_recv_sem,
):
    n_x, n_y, n_f, entries = sizes
    f_local, depth, sep = basis_ref.shape
    rhs_count = rhs_ref.shape[2]
    children = owner_ref.shape[1]
    rank = depth // children
    blocks = sep // BLOCK
    paired = n_x == 4
    x = lax.axis_index("sx")
    y = lax.axis_index("sy")
    z = lax.axis_index("freq")

    loads = []
    for f in range(f_local):
        loads.append(pltpu.make_async_copy(basis_hbm.at[f], basis_ref.at[f], basis_sem.at[f]))
    inverse_loads = []
    for f in range(f_local):
        inverse_loads.append(
            pltpu.make_async_copy(inverse_hbm.at[f], inverse_ref.at[f], inverse_sem.at[f])
        )
    for copy in loads + inverse_loads:
        copy.start()

    barrier = pltpu.get_barrier_semaphore()
    count = 0
    for dx in range(n_x):
        for dz in range(n_f):
            if dx or dz:
                pl.semaphore_signal(
                    barrier, inc=1, device_id=(lax.rem(x + dx, n_x), y, lax.rem(z + dz, n_f)),
                    device_id_type=MESH,
                )
                count += 1
    for dy in range(1, n_y):
        pl.semaphore_signal(
            barrier, inc=1, device_id=(x, lax.rem(y + dy, n_y), z), device_id_type=MESH
        )
        count += 1

    if paired:
        px, py = lax.rem(x, 2), x // 2
        owners = [(1 - py) * 2 + 1 - px, py * 2 + 1 - px, (1 - py) * 2 + px, x]
    else:
        owners = [lax.rem(x + k, n_x) for k in range(1, n_x)] + [x]

    child_of = lax.broadcasted_iota(jnp.int32, (children, depth), 1) // rank
    spread = (child_of == lax.broadcasted_iota(jnp.int32, (children, depth), 0)).astype(F32)
    owner_rows = jnp.broadcast_to(owner_ref[...].astype(F32), (8, children))
    owner_lanes = jnp.dot(
        owner_rows.astype(BF16), spread.astype(BF16), preferred_element_type=F32
    )[0:1, :]

    def mask(f):
        turned = coeff_ref[f].astype(F32).T
        for k, who in enumerate(owners):
            keep = jnp.where(owner_lanes == jnp.asarray(who).astype(F32), 1.0, 0.0)
            masked_ref[f, k * rhs_count:(k + 1) * rhs_count, :] = (turned * keep).astype(BF16)

    pending = []

    def remote(src, dst, send, recv, device):
        return pltpu.make_async_remote_copy(
            src_ref=src, dst_ref=dst, send_sem=send, recv_sem=recv,
            device_id=device, device_id_type=MESH,
        )

    def sum_copy(f, k, b):
        return remote(
            sent_ref.at[k, f, b], got_ref.at[k, f, b],
            sent_sem.at[k, f, b], got_sem.at[k, f, b], (owners[k], y, z),
        )

    for f in range(f_local):
        mask(f)
        loads[f].wait()
        for b in range(blocks):
            part = basis_ref[f, :, b * BLOCK:(b + 1) * BLOCK]
            for low in range(0, n_x * rhs_count, GROUP):
                high = min(low + GROUP, n_x * rhs_count)
                sums = jnp.dot(masked_ref[f, low:high, :], part, preferred_element_type=F32)
                for k in range(low // rhs_count, high // rhs_count):
                    at = k * rhs_count - low
                    piece = sums[at:at + rhs_count, :]
                    if k == n_x - 1:
                        own_ref[f, b] = piece
                    else:
                        sent_ref[k, f, b] = piece.astype(BF16)

    pl.semaphore_wait(barrier, count)
    for f in range(f_local):
        for b in range(blocks):
            for k in range(n_x - 1):
                copy = sum_copy(f, k, b)
                copy.start()
                pending.append((None, copy))

    both = jnp.concatenate([coupling_ref[f] for f in range(f_local)], axis=0)
    coupling_t_ref[...] = both.T

    edges = ((x == 0, 0), (x == n_x - 1, 1), (y == 0, 2), (y == n_y - 1, 3))
    for missing, side in edges:
        @pl.when(missing)
        def _():
            for sweep in range(SWEEPS):
                for f in range(f_local):
                    halo_in_ref[sweep, f, side] = jnp.zeros((sep, rhs_count), BF16)

    def halo_copy(sweep, f, b, way, source, device):
        rows = pl.ds(b * BLOCK, BLOCK)
        return remote(
            source, halo_in_ref.at[sweep, f, way, rows],
            halo_out_sem.at[sweep, f, way, b], halo_in_sem.at[sweep, f, way, b], device,
        )

    up, down = x < n_x - 1, x > 0
    if paired:
        up = jnp.logical_and(up, x != 1)
        down = jnp.logical_and(down, x != 2)

    def send_halo(sweep, f, b):
        source = halo_out_ref.at[sweep, f, pl.ds(b * BLOCK, BLOCK)]
        for way, test, device in (
            (0, up, (x + 1, y, z)), (1, down, (x - 1, y, z)),
            (2, y < n_y - 1, (x, y + 1, z)), (3, y > 0, (x, y - 1, z)),
        ):
            copy = halo_copy(sweep, f, b, way, source, device)
            pl.when(test)(copy.start)
            pending.append((test, copy))

    def wait_halo(sweep, f, b, way):
        source = halo_out_ref.at[sweep, f, pl.ds(b * BLOCK, BLOCK)]
        test = (x > 0, x < n_x - 1, y > 0, y < n_y - 1)[way]
        copy = halo_copy(sweep, f, b, way, source, (x, y, z))
        pl.when(test)(copy.wait_recv)

    def pass_on(sweep, f, b):
        rows = pl.ds(b * BLOCK, BLOCK)
        for test, held, way, target in ((x == 0, 1, 0, 2), (x == 3, 0, 1, 1)):
            source = halo_in_ref.at[sweep, f, held, rows]
            copy = remote(
                source, halo_in_ref.at[sweep, f, way, rows],
                halo_out_sem.at[sweep, f, held, b], halo_in_sem.at[sweep, f, way, b],
                (target, y, z),
            )
            pl.when(test)(copy.start)
            pending.append((test, copy))

    def apply_inverse(f, sweep, first):
        for b in range(blocks):
            rows = pl.ds(b * BLOCK, BLOCK)
            value = jnp.dot(inverse_ref[f, rows, :], field_ref[f], preferred_element_type=F32)
            if not first:
                value = out_ref[f, rows, :] + value
            out_ref[f, rows, :] = value
            if sweep < SWEEPS:
                halo_out_ref[sweep, f, rows, :] = value.astype(BF16)
                send_halo(sweep, f, b)

    for f in range(f_local):
        for b in range(blocks):
            rows = pl.ds(b * BLOCK, BLOCK)
            value = own_ref[f, b]
            for k in range(n_x - 1):
                sum_copy(f, k, b).wait_recv()
                value = value + got_ref[k, f, b].astype(F32)
            value = rhs_ref[f, rows, :].astype(F32) - value.T
            right_ref[f, rows, :] = value
            field_ref[f, rows, :] = value.astype(BF16)
        inverse_loads[f].wait()
        apply_inverse(f, 0, True)

    weighted = jnp.zeros((8, rhs_count), F32)
    for sweep in range(SWEEPS):
        for f in range(f_local):
            for b in range(blocks):
                wait_halo(sweep, f, b, 0)
                wait_halo(sweep, f, b, 1)
                if paired:
                    pass_on(sweep, f, b)
            squares = jnp.zeros((8, rhs_count), F32)
            for b in range(blocks):
                wait_halo(sweep, f, b, 2)
                wait_halo(sweep, f, b, 3)
                rows = pl.ds(b * BLOCK, BLOCK)
                beside = jnp.zeros((BLOCK, rhs_count), F32)
                for side in range(4):
                    column = 4 * f + side
                    beside = beside + (
                        coupling_t_ref[rows, column:column + 1]
                        * halo_in_ref[sweep, f, side, rows, :].astype(F32)
                    )
                residual = right_ref[f, rows, :] - out_ref[f, rows, :] + beside
                field_ref[f, rows, :] = residual.astype(BF16)
                if sweep == SWEEPS - 1:
                    squares = squares + jnp.sum(
                        (residual * residual).reshape(BLOCK // 8, 8, rhs_count), axis=0
                    )
            if sweep == SWEEPS - 1:
                weight = (z * f_local + f + 1).astype(F32)
                weighted = weighted + (weight * weight) * squares
                if f == f_local - 1:
                    mine = x * n_f + z
                    sums_a_ref[mine] = weighted
                    for dx in range(n_x):
                        for dz in range(n_f):
                            if dx or dz:
                                k = dx * n_f + dz
                                copy = remote(
                                    sums_a_ref.at[mine], sums_a_ref.at[mine],
                                    a_send_sem.at[k], a_recv_sem.at[k],
                                    (lax.rem(x + dx, n_x), y, lax.rem(z + dz, n_f)),
                                )
                                copy.start()
                                pending.append((None, copy))
            apply_inverse(f, sweep + 1, False)

    for k in range(1, n_x * n_f):
        dx, dz = k // n_f, k % n_f
        source = lax.rem(x + n_x - dx, n_x) * n_f + lax.rem(z + n_f - dz, n_f)
        remote(
            sums_a_ref.at[source], sums_a_ref.at[source], a_send_sem.at[k], a_recv_sem.at[k],
            (x, y, z),
        ).wait_recv()
    part = sums_a_ref[0]
    for k in range(1, n_x * n_f):
        part = part + sums_a_ref[k]
    sums_b_ref[y] = part
    for dy in range(1, n_y):
        copy = remote(
            sums_b_ref.at[y], sums_b_ref.at[y], b_send_sem.at[dy], b_recv_sem.at[dy],
            (x, lax.rem(y + dy, n_y), z),
        )
        copy.start()
        pending.append((None, copy))
    for dy in range(1, n_y):
        source = lax.rem(y + n_y - dy, n_y)
        remote(
            sums_b_ref.at[source], sums_b_ref.at[source], b_send_sem.at[dy], b_recv_sem.at[dy],
            (x, y, z),
        ).wait_recv()
    part = sums_b_ref[0]
    for k in range(1, n_y):
        part = part + sums_b_ref[k]
    whole = jnp.sum(jnp.sum(part, axis=1, keepdims=True), axis=0, keepdims=True)
    total_ref[...] = jnp.sqrt(whole / entries + 1e-06)

    for test, copy in pending:
        if test is None:
            copy.wait_send()
        else:
            pl.when(test)(copy.wait_send)


def on_device(sizes, update_basis, update_coeff, owner, sep_rhs, coupling, frontal_inverse):
    f_local, children, rank, sep = update_basis.shape
    rhs_count = update_coeff.shape[3]
    depth = children * rank
    n_x, n_y, n_f = sizes
    blocks = sep // BLOCK
    entries = float(f_local * n_f * n_x * n_y * sep * rhs_count)
    vmem = pl.BlockSpec(memory_space=pltpu.VMEM)
    anywhere = pl.BlockSpec(memory_space=pl.ANY)
    solved, total = pl.pallas_call(
        functools.partial(kernel, (n_x, n_y, n_f, entries)),
        out_shape=(
            jax.ShapeDtypeStruct((f_local, sep, rhs_count), F32),
            jax.ShapeDtypeStruct((1, 1), F32),
        ),
        in_specs=[anywhere, vmem, vmem, vmem, vmem, anywhere],
        out_specs=(vmem, vmem),
        scratch_shapes=[
            pltpu.VMEM((f_local, depth, sep), BF16),
            pltpu.VMEM((f_local, sep, sep), BF16),
            pltpu.VMEM((f_local, n_x * rhs_count, depth), BF16),
            pltpu.VMEM((n_x - 1, f_local, blocks, rhs_count, BLOCK), BF16),
            pltpu.VMEM((n_x - 1, f_local, blocks, rhs_count, BLOCK), BF16),
            pltpu.VMEM((f_local, blocks, rhs_count, BLOCK), F32),
            pltpu.VMEM((f_local, sep, rhs_count), F32),
            pltpu.VMEM((f_local, sep, rhs_count), BF16),
            pltpu.VMEM((SWEEPS, f_local, sep, rhs_count), BF16),
            pltpu.VMEM((SWEEPS, f_local, 4, sep, rhs_count), BF16),
            pltpu.VMEM((sep, 4 * f_local), F32),
            pltpu.VMEM((n_x * n_f, 8, rhs_count), F32),
            pltpu.VMEM((n_y, 8, rhs_count), F32),
            pltpu.SemaphoreType.DMA((f_local,)),
            pltpu.SemaphoreType.DMA((f_local,)),
            pltpu.SemaphoreType.DMA((n_x - 1, f_local, blocks)),
            pltpu.SemaphoreType.DMA((n_x - 1, f_local, blocks)),
            pltpu.SemaphoreType.DMA((SWEEPS, f_local, 4, blocks)),
            pltpu.SemaphoreType.DMA((SWEEPS, f_local, 4, blocks)),
            pltpu.SemaphoreType.DMA((n_x * n_f,)),
            pltpu.SemaphoreType.DMA((n_x * n_f,)),
            pltpu.SemaphoreType.DMA((n_y,)),
            pltpu.SemaphoreType.DMA((n_y,)),
        ],
        compiler_params=pltpu.CompilerParams(
            collective_id=0, has_side_effects=True, vmem_limit_bytes=56 * 2**20
        ),
    )(
        update_basis.reshape(f_local, depth, sep),
        update_coeff.reshape(f_local, depth, rhs_count),
        owner.reshape(1, children),
        sep_rhs[:, 0, 0],
        coupling[:, 0, 0],
        frontal_inverse[:, 0, 0],
    )
    return (solved[:, None, None], total.reshape(()))


def solution(mesh):
    sizes = (mesh.shape["sx"], mesh.shape["sy"], mesh.shape["freq"])
    return jax.shard_map(
        functools.partial(on_device, sizes),
        mesh=mesh,
        in_specs=(
            P("freq", ("sx", "sy"), None, None),
            P("freq", ("sx", "sy"), None, None),
            P(("sx", "sy"), None),
            P("freq", "sx", "sy", None, None),
            P("freq", "sx", "sy", None, None),
            P("freq", "sx", "sy", None, None),
        ),
        out_specs=(P("freq", "sx", "sy", None, None), P()),
        check_vma=False,
    )
```

```python
import functools
import jax
import jax.numpy as jnp
from jax import lax
from jax.experimental import pallas as pl
from jax.experimental.pallas import tpu as pltpu
from jax.sharding import PartitionSpec as P

SWEEPS = 2
BLOCK = 256
GROUP = 512
MESH = pl.DeviceIdType.MESH
F32 = jnp.float32
BF16 = jnp.bfloat16


def kernel(
    sizes,
    basis_hbm, coeff_ref, owner_ref, rhs_ref, coupling_ref, inverse_hbm,
    out_ref, total_ref,
    basis_ref, inverse_ref, masked_ref, sent_ref, got_ref, own_ref, right_ref, field_ref,
    halo_out_ref, halo_in_ref, coupling_t_ref, sums_a_ref, sums_b_ref,
    basis_sem, inverse_sem, sent_sem, got_sem, halo_out_sem, halo_in_sem,
    a_send_sem, a_recv_sem, b_send_sem, b_recv_sem,
):
    n_x, n_y, n_f, entries = sizes
    f_local, depth, sep = basis_ref.shape
    rhs_count = rhs_ref.shape[2]
    children = owner_ref.shape[1]
    rank = depth // children
    blocks = sep // BLOCK
    paired = n_x == 4
    x = lax.axis_index("sx")
    y = lax.axis_index("sy")
    z = lax.axis_index("freq")

    loads = []
    for f in range(f_local):
        loads.append(pltpu.make_async_copy(basis_hbm.at[f], basis_ref.at[f], basis_sem.at[f]))
    inverse_loads = []
    for f in range(f_local):
        inverse_loads.append(
            pltpu.make_async_copy(inverse_hbm.at[f], inverse_ref.at[f], inverse_sem.at[f])
        )
    for copy in loads + inverse_loads:
        copy.start()

    barrier = pltpu.get_barrier_semaphore()
    count = 0
    for dx in range(n_x):
        for dz in range(n_f):
            if dx or dz:
                pl.semaphore_signal(
                    barrier, inc=1, device_id=(lax.rem(x + dx, n_x), y, lax.rem(z + dz, n_f)),
                    device_id_type=MESH,
                )
                count += 1
    for dy in range(1, n_y):
        pl.semaphore_signal(
            barrier, inc=1, device_id=(x, lax.rem(y + dy, n_y), z), device_id_type=MESH
        )
        count += 1

    if paired:
        px, py = lax.rem(x, 2), x // 2
        owners = [(1 - py) * 2 + 1 - px, py * 2 + 1 - px, (1 - py) * 2 + px, x]
    else:
        owners = [lax.rem(x + k, n_x) for k in range(1, n_x)] + [x]

    child_of = lax.broadcasted_iota(jnp.int32, (children, depth), 1) // rank
    spread = (child_of == lax.broadcasted_iota(jnp.int32, (children, depth), 0)).astype(F32)
    owner_rows = jnp.broadcast_to(owner_ref[...].astype(F32), (8, children))
    owner_lanes = jnp.dot(
        owner_rows.astype(BF16), spread.astype(BF16), preferred_element_type=F32
    )[0:1, :]

    def mask(f):
        turned = coeff_ref[f].astype(F32).T
        for k, who in enumerate(owners):
            keep = jnp.where(owner_lanes == jnp.asarray(who).astype(F32), 1.0, 0.0)
            masked_ref[f, k * rhs_count:(k + 1) * rhs_count, :] = (turned * keep).astype(BF16)

    pending = []

    def remote(src, dst, send, recv, device):
        return pltpu.make_async_remote_copy(
            src_ref=src, dst_ref=dst, send_sem=send, recv_sem=recv,
            device_id=device, device_id_type=MESH,
        )

    def sum_copy(f, k, b):
        return remote(
            sent_ref.at[k, f, b], got_ref.at[k, f, b],
            sent_sem.at[k, f, b], got_sem.at[k, f, b], (owners[k], y, z),
        )

    for f in range(f_local):
        mask(f)
        loads[f].wait()
        if f == 0:
            pl.semaphore_wait(barrier, count)
        for b in range(blocks):
            part = basis_ref[f, :, b * BLOCK:(b + 1) * BLOCK]
            for low in range(0, n_x * rhs_count, GROUP):
                high = min(low + GROUP, n_x * rhs_count)
                sums = jnp.dot(masked_ref[f, low:high, :], part, preferred_element_type=F32)
                for k in range(low // rhs_count, high // rhs_count):
                    at = k * rhs_count - low
                    piece = sums[at:at + rhs_count, :]
                    if k == n_x - 1:
                        own_ref[f, b] = piece
                    else:
                        sent_ref[k, f, b] = piece.astype(BF16)
                        copy = sum_copy(f, k, b)
                        copy.start()
                        pending.append((None, copy))

    both = jnp.concatenate([coupling_ref[f] for f in range(f_local)], axis=0)
    coupling_t_ref[...] = both.T

    edges = ((x == 0, 0), (x == n_x - 1, 1), (y == 0, 2), (y == n_y - 1, 3))
    for missing, side in edges:
        @pl.when(missing)
        def _():
            for sweep in range(SWEEPS):
                for f in range(f_local):
                    halo_in_ref[sweep, f, side] = jnp.zeros((sep, rhs_count), BF16)

    def halo_copy(sweep, f, b, way, source, device):
        rows = pl.ds(b * BLOCK, BLOCK)
        return remote(
            source, halo_in_ref.at[sweep, f, way, rows],
            halo_out_sem.at[sweep, f, way, b], halo_in_sem.at[sweep, f, way, b], device,
        )

    up, down = x < n_x - 1, x > 0
    if paired:
        up = jnp.logical_and(up, x != 1)
        down = jnp.logical_and(down, x != 2)

    def send_halo(sweep, f, b):
        source = halo_out_ref.at[sweep, f, pl.ds(b * BLOCK, BLOCK)]
        for way, test, device in (
            (0, up, (x + 1, y, z)), (1, down, (x - 1, y, z)),
            (2, y < n_y - 1, (x, y + 1, z)), (3, y > 0, (x, y - 1, z)),
        ):
            copy = halo_copy(sweep, f, b, way, source, device)
            pl.when(test)(copy.start)
            pending.append((test, copy))

    def wait_halo(sweep, f, b, way):
        source = halo_out_ref.at[sweep, f, pl.ds(b * BLOCK, BLOCK)]
        test = (x > 0, x < n_x - 1, y > 0, y < n_y - 1)[way]
        copy = halo_copy(sweep, f, b, way, source, (x, y, z))
        pl.when(test)(copy.wait_recv)

    def pass_on(sweep, f, b):
        rows = pl.ds(b * BLOCK, BLOCK)
        for test, held, way, target in ((x == 0, 1, 0, 2), (x == 3, 0, 1, 1)):
            source = halo_in_ref.at[sweep, f, held, rows]
            copy = remote(
                source, halo_in_ref.at[sweep, f, way, rows],
                halo_out_sem.at[sweep, f, held, b], halo_in_sem.at[sweep, f, way, b],
                (target, y, z),
            )
            pl.when(test)(copy.start)
            pending.append((test, copy))

    def apply_inverse(f, sweep, first):
        for b in range(blocks):
            rows = pl.ds(b * BLOCK, BLOCK)
            value = jnp.dot(inverse_ref[f, rows, :], field_ref[f], preferred_element_type=F32)
            if not first:
                value = out_ref[f, rows, :] + value
            out_ref[f, rows, :] = value
            if sweep < SWEEPS:
                halo_out_ref[sweep, f, rows, :] = value.astype(BF16)
                send_halo(sweep, f, b)

    for f in range(f_local):
        for b in range(blocks):
            rows = pl.ds(b * BLOCK, BLOCK)
            value = own_ref[f, b]
            for k in range(n_x - 1):
                sum_copy(f, k, b).wait_recv()
                value = value + got_ref[k, f, b].astype(F32)
            value = rhs_ref[f, rows, :].astype(F32) - value.T
            right_ref[f, rows, :] = value
            field_ref[f, rows, :] = value.astype(BF16)
        inverse_loads[f].wait()
        apply_inverse(f, 0, True)

    weighted = jnp.zeros((8, rhs_count), F32)
    for sweep in range(SWEEPS):
        for f in range(f_local):
            for b in range(blocks):
                wait_halo(sweep, f, b, 0)
                wait_halo(sweep, f, b, 1)
                if paired:
                    pass_on(sweep, f, b)
            squares = jnp.zeros((8, rhs_count), F32)
            for b in range(blocks):
                wait_halo(sweep, f, b, 2)
                wait_halo(sweep, f, b, 3)
                rows = pl.ds(b * BLOCK, BLOCK)
                beside = jnp.zeros((BLOCK, rhs_count), F32)
                for side in range(4):
                    column = 4 * f + side
                    beside = beside + (
                        coupling_t_ref[rows, column:column + 1]
                        * halo_in_ref[sweep, f, side, rows, :].astype(F32)
                    )
                residual = right_ref[f, rows, :] - out_ref[f, rows, :] + beside
                field_ref[f, rows, :] = residual.astype(BF16)
                if sweep == SWEEPS - 1:
                    squares = squares + jnp.sum(
                        (residual * residual).reshape(BLOCK // 8, 8, rhs_count), axis=0
                    )
            if sweep == SWEEPS - 1:
                weight = (z * f_local + f + 1).astype(F32)
                weighted = weighted + (weight * weight) * squares
                if f == f_local - 1:
                    mine = x * n_f + z
                    sums_a_ref[mine] = weighted
                    for dx in range(n_x):
                        for dz in range(n_f):
                            if dx or dz:
                                k = dx * n_f + dz
                                copy = remote(
                                    sums_a_ref.at[mine], sums_a_ref.at[mine],
                                    a_send_sem.at[k], a_recv_sem.at[k],
                                    (lax.rem(x + dx, n_x), y, lax.rem(z + dz, n_f)),
                                )
                                copy.start()
                                pending.append((None, copy))
            apply_inverse(f, sweep + 1, False)

    for k in range(1, n_x * n_f):
        dx, dz = k // n_f, k % n_f
        source = lax.rem(x + n_x - dx, n_x) * n_f + lax.rem(z + n_f - dz, n_f)
        remote(
            sums_a_ref.at[source], sums_a_ref.at[source], a_send_sem.at[k], a_recv_sem.at[k],
            (x, y, z),
        ).wait_recv()
    part = sums_a_ref[0]
    for k in range(1, n_x * n_f):
        part = part + sums_a_ref[k]
    sums_b_ref[y] = part
    for dy in range(1, n_y):
        copy = remote(
            sums_b_ref.at[y], sums_b_ref.at[y], b_send_sem.at[dy], b_recv_sem.at[dy],
            (x, lax.rem(y + dy, n_y), z),
        )
        copy.start()
        pending.append((None, copy))
    for dy in range(1, n_y):
        source = lax.rem(y + n_y - dy, n_y)
        remote(
            sums_b_ref.at[source], sums_b_ref.at[source], b_send_sem.at[dy], b_recv_sem.at[dy],
            (x, y, z),
        ).wait_recv()
    part = sums_b_ref[0]
    for k in range(1, n_y):
        part = part + sums_b_ref[k]
    whole = jnp.sum(jnp.sum(part, axis=1, keepdims=True), axis=0, keepdims=True)
    total_ref[...] = jnp.sqrt(whole / entries + 1e-06)

    for test, copy in pending:
        if test is None:
            copy.wait_send()
        else:
            pl.when(test)(copy.wait_send)


def on_device(sizes, update_basis, update_coeff, owner, sep_rhs, coupling, frontal_inverse):
    f_local, children, rank, sep = update_basis.shape
    rhs_count = update_coeff.shape[3]
    depth = children * rank
    n_x, n_y, n_f = sizes
    blocks = sep // BLOCK
    entries = float(f_local * n_f * n_x * n_y * sep * rhs_count)
    vmem = pl.BlockSpec(memory_space=pltpu.VMEM)
    anywhere = pl.BlockSpec(memory_space=pl.ANY)
    solved, total = pl.pallas_call(
        functools.partial(kernel, (n_x, n_y, n_f, entries)),
        out_shape=(
            jax.ShapeDtypeStruct((f_local, sep, rhs_count), F32),
            jax.ShapeDtypeStruct((1, 1), F32),
        ),
        in_specs=[anywhere, vmem, vmem, vmem, vmem, anywhere],
        out_specs=(vmem, vmem),
        scratch_shapes=[
            pltpu.VMEM((f_local, depth, sep), BF16),
            pltpu.VMEM((f_local, sep, sep), BF16),
            pltpu.VMEM((f_local, n_x * rhs_count, depth), BF16),
            pltpu.VMEM((n_x - 1, f_local, blocks, rhs_count, BLOCK), BF16),
            pltpu.VMEM((n_x - 1, f_local, blocks, rhs_count, BLOCK), BF16),
            pltpu.VMEM((f_local, blocks, rhs_count, BLOCK), F32),
            pltpu.VMEM((f_local, sep, rhs_count), F32),
            pltpu.VMEM((f_local, sep, rhs_count), BF16),
            pltpu.VMEM((SWEEPS, f_local, sep, rhs_count), BF16),
            pltpu.VMEM((SWEEPS, f_local, 4, sep, rhs_count), BF16),
            pltpu.VMEM((sep, 4 * f_local), F32),
            pltpu.VMEM((n_x * n_f, 8, rhs_count), F32),
            pltpu.VMEM((n_y, 8, rhs_count), F32),
            pltpu.SemaphoreType.DMA((f_local,)),
            pltpu.SemaphoreType.DMA((f_local,)),
            pltpu.SemaphoreType.DMA((n_x - 1, f_local, blocks)),
            pltpu.SemaphoreType.DMA((n_x - 1, f_local, blocks)),
            pltpu.SemaphoreType.DMA((SWEEPS, f_local, 4, blocks)),
            pltpu.SemaphoreType.DMA((SWEEPS, f_local, 4, blocks)),
            pltpu.SemaphoreType.DMA((n_x * n_f,)),
            pltpu.SemaphoreType.DMA((n_x * n_f,)),
            pltpu.SemaphoreType.DMA((n_y,)),
            pltpu.SemaphoreType.DMA((n_y,)),
        ],
        compiler_params=pltpu.CompilerParams(
            collective_id=0, has_side_effects=True, vmem_limit_bytes=56 * 2**20
        ),
    )(
        update_basis.reshape(f_local, depth, sep),
        update_coeff.reshape(f_local, depth, rhs_count),
        owner.reshape(1, children),
        sep_rhs[:, 0, 0],
        coupling[:, 0, 0],
        frontal_inverse[:, 0, 0],
    )
    return (solved[:, None, None], total.reshape(()))


def solution(mesh):
    sizes = (mesh.shape["sx"], mesh.shape["sy"], mesh.shape["freq"])
    return jax.shard_map(
        functools.partial(on_device, sizes),
        mesh=mesh,
        in_specs=(
            P("freq", ("sx", "sy"), None, None),
            P("freq", ("sx", "sy"), None, None),
            P(("sx", "sy"), None),
            P("freq", "sx", "sy", None, None),
            P("freq", "sx", "sy", None, None),
            P("freq", "sx", "sy", None, None),
        ),
        out_specs=(P("freq", "sx", "sy", None, None), P()),
        check_vma=False,
    )
```
